32 devices in a mesh: groups: 2 (over x), vocab: 8 (over z, y), seq: 2 (over core).
Axes of the slice: x: 2, y: 2, z: 4, core: 2. Of those that a mesh axis runs over, the one named last changes fastest.
Arguments:
- out_grad: bfloat16 [6144, 4096], P(('groups', 'vocab', 'seq')), parts along dimension 0, may hold values from -1.5 to 1.5
- token_ids: int32 [6144], P(('groups', 'vocab', 'seq')), parts along dimension 0, may hold values from 0 to 3583
- table: float32 [7168, 4096], P(('groups', 'vocab'), 'seq'), parts along dimension 0, may hold values from -6 to 6
- moment1: float32 [7168, 4096], P(('groups', 'vocab'), 'seq'), parts along dimension 0, may hold values from -1.8 to 1.8
- moment2: float32 [7168, 4096], P(('groups', 'vocab'), 'seq'), parts along dimension 0, may hold values from 0.01 to 1
Outputs:
- new_table: float32 [7168, 4096], P(('groups', 'vocab'), 'seq'), parts along dimension 0
- new_moment1: float32 [7168, 4096], P(('groups', 'vocab'), 'seq'), parts along dimension 0
- new_moment2: float32 [7168, 4096], P(('groups', 'vocab'), 'seq'), parts along dimension 0
The draws below stay inside these ranges and needn't reach their ends.
There are 2 independent parts, one for each index of `groups`. The reference program is written for one: setup_inputs(seed, part) draws one part's arguments, and reference() takes and returns one part's arrays. A program takes and returns all parts, laid end to end along the dimension named above; each array names one. Nothing has to cross between parts.
All inputs are finite; a program needn't handle non-finite values.
Results may differ from the reference program's by a relative error of at most 0.00065.
Values may be sent and summed in bfloat16 or wider, within the bound.
A program may use at most 128 MiB of HBM per device.

```python
import math
import jax
import jax.numpy as jnp
import numpy as np

D = 4096
STEP = 10
VOCAB = 3584
TOKENS = 3072


def place_ends(array, rng, smallest, largest):
    dims = array.shape
    place = [jax.random.randint(jax.random.fold_in(rng, axis), (), 0, dims[axis]) for axis in range(len(dims))]
    array = array.at[tuple(place)].set(smallest)
    longest = dims.index(max(dims))
    place[longest] = (place[longest] + 1) % dims[longest]
    return array.at[tuple(place)].set(largest)


def steps_of(rng, shape, shards, smallest, top_value):
    level, own = 1.0, jax.random.fold_in(rng, 6)
    for axis_at, parts in shards:
        draws = jnp.exp(jax.random.uniform(jax.random.fold_in(own, axis_at), (parts,), jnp.float32, smallest / len(shards), top_value / len(shards)))
        level = level * jnp.repeat(draws, shape[axis_at] // parts).reshape([-1 if axis == axis_at else 1 for axis in range(len(shape))])
    return level


def cumulative_ranks(amount, slope):
    weights = [(1 << 20) // math.isqrt(grade ** slope) + 1 for grade in range(1, amount + 1)]
    deviation = 1 + sum(weights) // (1 << 30)
    return np.cumsum(np.array([max(1, weight // deviation) for weight in weights]))


def skewed_ids(own_key, shape, amount, lean):
    listing = cumulative_ranks(amount, lean)
    lot = jax.random.randint(jax.random.fold_in(own_key, 1), shape, 0, int(listing[amount - 1]))
    rank = jnp.searchsorted(jnp.asarray(listing, jnp.int32), lot, side="right")
    return jax.random.permutation(jax.random.fold_in(own_key, 2), amount)[rank].astype(jnp.int32)


def scatter_about(stream_key, shape, spread, reach, split=(), kind=jnp.bfloat16):
    gain = steps_of(stream_key, shape, split, -0.22, 0.18) if split else 1.0
    values = jax.random.normal(stream_key, shape, jnp.float32) * spread * gain
    return jnp.minimum(jnp.maximum(values, -reach), reach).astype(kind)


def setup_inputs(seed: int = 0, part: int = 0) -> dict:
    key_of = jax.random.split(jax.random.key(seed), 6)
    part_keys = jax.random.split(jax.random.fold_in(key_of[5], part), 6)
    return {
        "out_grad": scatter_about(part_keys[0], (TOKENS, D), 0.25, 1.5, ((0, 16),)),
        "token_ids": place_ends(skewed_ids(part_keys[1], (TOKENS,), VOCAB, 2), jax.random.fold_in(part_keys[1], 3), 0, VOCAB - 1).astype(jnp.int32),
        "table": scatter_about(part_keys[2], (VOCAB, D), 1.0, 6.0, ((0, 8), (1, 2)), jnp.float32),
        "moment1": scatter_about(part_keys[3], (VOCAB, D), 0.3, 1.8, ((0, 8), (1, 2)), jnp.float32),
        "moment2": jnp.clip(jnp.exp(math.log(1.0) - 4.6051702 * jax.random.uniform(part_keys[4], (VOCAB, D), jnp.float32) ** steps_of(part_keys[4], (VOCAB, D), ((0, 8), (1, 2)), -0.2, 0.2)), 0.01, 1.0),
    }


def reference(out_grad, token_ids, table, moment1, moment2):
    grad = jax.ops.segment_sum(out_grad.astype(jnp.float32), token_ids, num_segments=VOCAB)
    new_moment1 = 0.9 * moment1 + 0.1 * grad
    new_moment2 = 0.999 * moment2 + 0.001 * grad * grad
    first_fix = 1.0 - 0.9 ** STEP
    second_fix = 1.0 - 0.999 ** STEP
    new_table = table - 0.001 * (new_moment1 / first_fix) / (jnp.sqrt(new_moment2 / second_fix) + 1e-08)
    return (new_table, new_moment1, new_moment2)
```

```python
import functools

import jax
import jax.numpy as jnp
from jax import lax
from jax.experimental import pallas as pl
from jax.experimental.pallas import tpu as pltpu
from jax.sharding import PartitionSpec as P

STEP = 10
BLOCK_ROWS = 48
LANES = 128
FIRST_FIX = 1.0 - 0.9**STEP
SECOND_FIX = 1.0 - 0.999**STEP
MESH = pl.DeviceIdType.MESH


def adam(grad, table, moment1, moment2):
    new_moment1 = 0.9 * moment1 + 0.1 * grad
    new_moment2 = 0.999 * moment2 + 0.001 * grad * grad
    new_table = table - 0.001 * (new_moment1 / FIRST_FIX) / (
        jnp.sqrt(new_moment2 / SECOND_FIX) + 1e-08
    )
    return new_table, new_moment1, new_moment2


def dense_update(out_grad, token_ids, table, moment1, moment2):
    slab_rows = table.shape[0]
    slab_ids = lax.axis_index("vocab") * slab_rows + lax.iota(jnp.int32, slab_rows)
    grad_rows = lax.all_gather(out_grad, "vocab", axis=0, tiled=True)
    row_ids = lax.all_gather(token_ids, "vocab", axis=0, tiled=True)
    onehot = (slab_ids[:, None] == row_ids[None, :]).astype(jnp.bfloat16)
    partial_value = jnp.dot(onehot, grad_rows, preferred_element_type=jnp.float32)
    grad = lax.psum_scatter(
        partial_value.astype(jnp.bfloat16), "seq", scatter_dimension=1, tiled=True
    ).astype(jnp.float32)
    return adam(grad, table, moment1, moment2)


def find_slots(ids, slabs, slab_rows):
    tokens = ids.shape[1]
    row = lax.broadcasted_iota(jnp.int32, (tokens, tokens), 0)
    lane = lax.broadcasted_iota(jnp.int32, (tokens, tokens), 1)

    def slab_of(values):
        slab = jnp.zeros_like(values)
        for k in range(1, slabs):
            slab += jnp.where(values >= float(k * slab_rows), 1.0, 0.0)
        return slab

    ids_down = jnp.sum(jnp.where(row == lane, ids, 0.0), axis=1, keepdims=True)
    same = ids_down == ids
    repeat_down = jnp.max(jnp.where(same & (lane < row), 1.0, 0.0), axis=1, keepdims=True)
    repeat = jnp.max(jnp.where(same & (row < lane), 1.0, 0.0), axis=0, keepdims=True)
    slab_down = slab_of(ids_down)
    slab_first = jnp.where((repeat == 0.0) & (ids >= 0.0), slab_of(ids), -1.0)
    first_down = (repeat_down == 0.0) & (ids_down >= 0.0)
    rank_down = jnp.sum(
        jnp.where((slab_down == slab_first) & (lane < row), 1.0, 0.0), axis=1, keepdims=True
    )
    most = jnp.max(jnp.where(first_down, rank_down + 1.0, 0.0), axis=0, keepdims=True)
    slot_down = jnp.where(
        first_down & (rank_down < float(BLOCK_ROWS)),
        slab_down * float(BLOCK_ROWS) + rank_down,
        -1.0,
    )
    slot = jnp.sum(jnp.where(same, slot_down + 1.0, 0.0), axis=0, keepdims=True) - 1.0
    return slot, slot_down, ids_down, most


def route_kernel(
    groups, slabs, slab_rows,
    ids_ref, grad_ref,
    got_ref, got_ids_ref, most_ref,
    rows_ref, other_ids_ref, send_ref, note_ref, got_note_ref, count_ref, got_count_ref,
    local_sem, pair_send, pair_recv, count_send, count_recv,
    note_send, note_recv, block_send, block_recv,
):
    tokens, width = grad_ref.shape
    half = width // 2
    padded = ids_ref.shape[1]
    slots = slabs * BLOCK_ROWS
    group, me, core = lax.axis_index("groups"), lax.axis_index("vocab"), lax.axis_index("seq")
    sibling = (group, me, 1 - core)
    twins = [(lax.rem(group + d, groups), me, core) for d in range(1, groups)]
    peers = [lax.rem(me + d, slabs) for d in range(1, slabs)]

    barrier = pltpu.get_barrier_semaphore()
    for device in [sibling] + twins + [(group, peer, core) for peer in peers]:
        pl.semaphore_signal(barrier, inc=1, device_id=device, device_id_type=MESH)
    pl.semaphore_wait(barrier, groups + slabs - 1)

    def columns(which):
        return pl.ds(pl.multiple_of(which * half, half), half)

    place = pl.ds(pl.multiple_of(core * padded, padded), tokens)
    ids_copy = pltpu.make_async_remote_copy(
        ids_ref, other_ids_ref, pair_send.at[0], pair_recv.at[0],
        device_id=sibling, device_id_type=MESH,
    )
    ids_copy.start()
    rows_copy = pltpu.make_async_remote_copy(
        grad_ref.at[:, columns(1 - core)], rows_ref.at[place], pair_send.at[1], pair_recv.at[1],
        device_id=sibling, device_id_type=MESH,
    )
    rows_copy.start()
    own_rows = pltpu.make_async_copy(grad_ref.at[:, columns(core)], rows_ref.at[place], local_sem.at[0])
    own_rows.start()
    for start in (0, padded):
        if padded > tokens:
            rows_ref[start + tokens : start + padded] = jnp.zeros(
                (padded - tokens, half), rows_ref.dtype
            )

    ids_copy.wait()
    mine, other = ids_ref[0:1, :], other_ids_ref[0:1, :]
    ids = jnp.concatenate(
        [jnp.where(core == 0, mine, other), jnp.where(core == 0, other, mine)], axis=1
    ).astype(jnp.float32)
    slot, slot_down, ids_down, most = find_slots(ids, slabs, slab_rows)

    count_ref[...] = jnp.broadcast_to(most.astype(jnp.int32), count_ref.shape)
    count_copies = []
    for d, twin in enumerate(twins):
        copy = pltpu.make_async_remote_copy(
            count_ref, got_count_ref.at[d], count_send.at[d], count_recv.at[d],
            device_id=twin, device_id_type=MESH,
        )
        copy.start()
        count_copies.append(copy)

    gather = (
        lax.broadcasted_iota(jnp.int32, (slots, 2 * padded), 0) == slot.astype(jnp.int32)
    ).astype(jnp.float32).astype(jnp.bfloat16)
    own_rows.wait()
    rows_copy.wait()
    step = min(half, 512)

    @pl.loop(0, half // step)
    def _(c):
        at = pl.ds(pl.multiple_of(c * step, step), step)
        send_ref[:, at] = jnp.dot(
            gather, rows_ref[:, at], preferred_element_type=jnp.float32
        ).astype(jnp.bfloat16)

    def block(k):
        return pl.ds(pl.multiple_of(k * BLOCK_ROWS, BLOCK_ROWS), BLOCK_ROWS)

    block_copies = []
    for d, peer in enumerate(peers):
        copy = pltpu.make_async_remote_copy(
            send_ref.at[block(peer)], got_ref.at[block(me)], block_send.at[d], block_recv.at[d],
            device_id=(group, peer, core), device_id_type=MESH,
        )
        copy.start()
        block_copies.append(copy)
    own_block = pltpu.make_async_copy(
        send_ref.at[block(me)], got_ref.at[block(me)], local_sem.at[1]
    )
    own_block.start()

    for d, copy in enumerate(count_copies):
        copy.wait()
        most = jnp.maximum(most, got_count_ref[d, 0:1, 0:1].astype(jnp.float32))
    lane = lax.broadcasted_iota(jnp.int32, (2 * padded, LANES), 1)
    sub = lax.broadcasted_iota(jnp.int32, (8, LANES), 0)
    slot_down = slot_down.astype(jnp.int32)
    for k in range(slabs):
        chosen = (slot_down == lane + k * BLOCK_ROWS) & (lane < BLOCK_ROWS)
        note = jnp.sum(jnp.where(chosen, ids_down + 1.0, 0.0), axis=0, keepdims=True) - 1.0
        note_ref[k] = jnp.where(sub == 0, note, most).astype(jnp.int32)
    note_copies = []
    for d, peer in enumerate(peers):
        copy = pltpu.make_async_remote_copy(
            note_ref.at[peer], got_note_ref.at[me], note_send.at[d], note_recv.at[d],
            device_id=(group, peer, core), device_id_type=MESH,
        )
        copy.start()
        note_copies.append(copy)
    own_note = pltpu.make_async_copy(note_ref.at[me], got_note_ref.at[me], local_sem.at[2])
    own_note.start()
    own_note.wait()
    for copy in note_copies:
        copy.wait()

    row = lax.broadcasted_iota(jnp.int32, (BLOCK_ROWS, LANES), 0)
    lane = lax.broadcasted_iota(jnp.int32, (BLOCK_ROWS, LANES), 1)
    wide_row = lax.broadcasted_iota(jnp.int32, (BLOCK_ROWS, slots), 0)
    wide_lane = lax.broadcasted_iota(jnp.int32, (BLOCK_ROWS, slots), 1)
    got_ids = jnp.zeros((1, slots), jnp.float32)
    for k in range(slabs):
        note = got_note_ref[k].astype(jnp.float32)
        most = jnp.maximum(most, note[1:2, 0:1])
        down = jnp.sum(jnp.where(row == lane, note[0:1], 0.0), axis=1, keepdims=True)
        got_ids += jnp.sum(
            jnp.where(wide_lane == wide_row + k * BLOCK_ROWS, down, 0.0), axis=0, keepdims=True
        )
    got_ids_ref[...] = jnp.broadcast_to(got_ids.astype(jnp.int32), got_ids_ref.shape)
    most_ref[...] = jnp.broadcast_to(most.astype(jnp.int32), most_ref.shape)

    own_block.wait()
    for copy in block_copies:
        copy.wait()


def route(out_grad, token_ids, groups, slabs, slab_rows):
    tokens, width = out_grad.shape
    padded = -(-tokens // LANES) * LANES
    slots = slabs * BLOCK_ROWS
    half = width // 2
    ids = jnp.pad(token_ids, (0, padded - tokens), constant_values=-1)
    ids = jnp.broadcast_to(ids[None, :], (8, padded))
    vmem = pl.BlockSpec(memory_space=pltpu.VMEM)
    anywhere = pl.BlockSpec(memory_space=pl.ANY)
    dma = pltpu.SemaphoreType.DMA
    others = max(groups - 1, 1)
    return pl.pallas_call(
        functools.partial(route_kernel, groups, slabs, slab_rows),
        out_shape=(
            jax.ShapeDtypeStruct((slots, half), jnp.bfloat16),
            jax.ShapeDtypeStruct((8, slots), jnp.int32),
            jax.ShapeDtypeStruct((8, LANES), jnp.int32),
        ),
        in_specs=[vmem, anywhere],
        out_specs=(anywhere, vmem, vmem),
        scratch_shapes=[
            pltpu.VMEM((2 * padded, half), jnp.bfloat16),
            pltpu.VMEM((8, padded), jnp.int32),
            pltpu.VMEM((slots, half), jnp.bfloat16),
            pltpu.VMEM((slabs, 8, LANES), jnp.int32),
            pltpu.VMEM((slabs, 8, LANES), jnp.int32),
            pltpu.VMEM((8, LANES), jnp.int32),
            pltpu.VMEM((others, 8, LANES), jnp.int32),
            dma((3,)),
            dma((2,)),
            dma((2,)),
            dma((others,)),
            dma((others,)),
            dma((slabs - 1,)),
            dma((slabs - 1,)),
            dma((slabs - 1,)),
            dma((slabs - 1,)),
        ],
        compiler_params=pltpu.CompilerParams(
            collective_id=0, has_side_effects=True, vmem_limit_bytes=24 * 1024 * 1024
        ),
        cost_estimate=pl.CostEstimate(
            flops=4 * slots * padded * half, bytes_accessed=60_000_000, transcendentals=0
        ),
        name="route_rows",
    )(ids, out_grad)


def adam_kernel(ids_ref, got_ref, table_ref, m1_ref, m2_ref, t_out, m1_out, m2_out, onehot_ref):
    slab_rows = table_ref.shape[0]

    @pl.when(pl.program_id(0) == 0)
    def _():
        first = lax.axis_index("vocab") * slab_rows
        row = lax.broadcasted_iota(jnp.int32, onehot_ref.shape, 0) + first
        onehot_ref[...] = (
            (row == ids_ref[0:1, :]).astype(jnp.float32).astype(jnp.bfloat16)
        )

    grad = jnp.dot(onehot_ref[...], got_ref[...], preferred_element_type=jnp.float32)
    t_out[...], m1_out[...], m2_out[...] = adam(grad, table_ref[...], m1_ref[...], m2_ref[...])


def update(got, got_ids, table, moment1, moment2):
    slab_rows, half = table.shape
    slots = got.shape[0]
    step = min(half, 256)
    tile = pl.BlockSpec((slab_rows, step), lambda c: (0, c))
    shape = jax.ShapeDtypeStruct(table.shape, jnp.float32)
    return pl.pallas_call(
        adam_kernel,
        grid=(half // step,),
        out_shape=(shape,) * 3,
        in_specs=[
            pl.BlockSpec((8, slots), lambda c: (0, 0)),
            pl.BlockSpec((slots, step), lambda c: (0, c)),
            tile, tile, tile,
        ],
        out_specs=(tile,) * 3,
        scratch_shapes=[pltpu.VMEM((slab_rows, slots), jnp.bfloat16)],
        compiler_params=pltpu.CompilerParams(vmem_limit_bytes=16 * 1024 * 1024),
        cost_estimate=pl.CostEstimate(
            flops=2 * slab_rows * slots * half,
            bytes_accessed=24 * slab_rows * half,
            transcendentals=slab_rows * half,
        ),
        name="adam_update",
    )(got_ids, got, table, moment1, moment2)


def per_device(groups, slabs, out_grad, token_ids, table, moment1, moment2):
    got, got_ids, most = route(out_grad, token_ids, groups, slabs, table.shape[0])
    outs = update(got, got_ids, table, moment1, moment2)

    def again(carry):
        return (jnp.int32(0),) + dense_update(out_grad, token_ids, table, moment1, moment2)

    return lax.while_loop(lambda carry: carry[0] > BLOCK_ROWS, again, (most[0, 0],) + tuple(outs))[1:]


def solution(mesh):
    slab = P(("groups", "vocab"), "seq")
    return jax.shard_map(
        functools.partial(per_device, mesh.shape["groups"], mesh.shape["vocab"]),
        mesh=mesh,
        in_specs=(
            P(("groups", "vocab", "seq"), None), P(("groups", "vocab", "seq")), slab, slab, slab,
        ),
        out_specs=(slab, slab, slab),
        check_vma=False,
    )
```

```python
import functools

import jax
import jax.numpy as jnp
from jax import lax
from jax.experimental import pallas as pl
from jax.experimental.pallas import tpu as pltpu
from jax.sharding import PartitionSpec as P

STEP = 10
BLOCK_ROWS = 48
LANES = 128
FIRST_FIX = 1.0 - 0.9**STEP
SECOND_FIX = 1.0 - 0.999**STEP
MESH = pl.DeviceIdType.MESH


def adam(grad, table, moment1, moment2):
    new_moment1 = 0.9 * moment1 + 0.1 * grad
    new_moment2 = 0.999 * moment2 + 0.001 * grad * grad
    new_table = table - new_moment1 * (0.001 / FIRST_FIX) / (
        jnp.sqrt(new_moment2 * (1.0 / SECOND_FIX)) + 1e-08
    )
    return new_table, new_moment1, new_moment2


def dense_update(out_grad, token_ids, table, moment1, moment2):
    slab_rows = table.shape[0]
    slab_ids = lax.axis_index("vocab") * slab_rows + lax.iota(jnp.int32, slab_rows)
    grad_rows = lax.all_gather(out_grad, "vocab", axis=0, tiled=True)
    row_ids = lax.all_gather(token_ids, "vocab", axis=0, tiled=True)
    onehot = (slab_ids[:, None] == row_ids[None, :]).astype(jnp.bfloat16)
    partial_value = jnp.dot(onehot, grad_rows, preferred_element_type=jnp.float32)
    grad = lax.psum_scatter(
        partial_value.astype(jnp.bfloat16), "seq", scatter_dimension=1, tiled=True
    ).astype(jnp.float32)
    return adam(grad, table, moment1, moment2)


def find_slots(ids, slabs, slab_rows):
    tokens = ids.shape[1]
    row = lax.broadcasted_iota(jnp.int32, (tokens, tokens), 0)
    lane = lax.broadcasted_iota(jnp.int32, (tokens, tokens), 1)
    ids_down = jnp.sum(jnp.where(row == lane, ids, 0.0), axis=1, keepdims=True)
    same = jnp.where(ids_down == ids, 1.0, 0.0)
    before = jnp.where(row < lane, 1.0, 0.0)
    first = 1.0 - jnp.max(same * before, axis=0, keepdims=True)
    slab = jnp.zeros_like(ids)
    for k in range(1, slabs):
        slab += jnp.where(ids >= float(k * slab_rows), 1.0, 0.0)

    member = jnp.where(
        slab == lax.broadcasted_iota(jnp.int32, (slabs, tokens), 0).astype(jnp.float32), first, 0.0
    )
    ahead = jnp.dot(
        member.astype(jnp.bfloat16), before.astype(jnp.bfloat16),
        preferred_element_type=jnp.float32,
    )
    rank = jnp.sum(member * ahead, axis=0, keepdims=True)
    most = jnp.max(first * (rank + 1.0), axis=1, keepdims=True)
    fits = jnp.where(rank < float(BLOCK_ROWS), first, 0.0)
    slot_first = fits * (slab * float(BLOCK_ROWS) + rank + 1.0) - 1.0

    field = lax.broadcasted_iota(jnp.int32, (8, tokens), 0)
    facts = jnp.where(
        field == 0, fits * slab, jnp.where(field == 1, fits * rank, jnp.where(field == 2, fits, 0.0))
    )
    facts = jnp.dot(
        facts.astype(jnp.bfloat16), same.astype(jnp.bfloat16), preferred_element_type=jnp.float32
    )
    slot = facts[0:1] * float(BLOCK_ROWS) + facts[1:2] + facts[2:3] - 1.0
    return slot, slot_first, ids_down, most


def route_kernel(
    groups, slabs, slab_rows,
    ids_ref, grad_ref, table_ref, m1_ref, m2_ref,
    got_ref, got_ids_ref, most_ref, near_table, near_m1, near_m2,
    rows_ref, other_ids_ref, send_ref, note_ref, got_note_ref, count_ref, got_count_ref,
    local_sem, near_sem, pair_send, pair_recv, count_send, count_recv,
    note_send, note_recv, block_send, block_recv,
):
    tokens, width = grad_ref.shape
    half = width // 2
    slots = slabs * BLOCK_ROWS
    group, me, core = lax.axis_index("groups"), lax.axis_index("vocab"), lax.axis_index("seq")
    sibling = (group, me, 1 - core)
    twins = [(lax.rem(group + d, groups), me, core) for d in range(1, groups)]
    peers = [lax.rem(me + d, slabs) for d in range(1, slabs)]

    barrier = pltpu.get_barrier_semaphore()
    for device in [sibling] + twins + [(group, peer, core) for peer in peers]:
        pl.semaphore_signal(barrier, inc=1, device_id=device, device_id_type=MESH)
    pl.semaphore_wait(barrier, groups + slabs - 1)

    def columns(which):
        return pl.ds(pl.multiple_of(which * half, half), half)

    place = pl.ds(pl.multiple_of(core * tokens, tokens), tokens)
    ids_copy = pltpu.make_async_remote_copy(
        ids_ref, other_ids_ref, pair_send.at[0], pair_recv.at[0],
        device_id=sibling, device_id_type=MESH,
    )
    ids_copy.start()
    rows_copy = pltpu.make_async_remote_copy(
        grad_ref.at[:, columns(1 - core)], rows_ref.at[place], pair_send.at[1], pair_recv.at[1],
        device_id=sibling, device_id_type=MESH,
    )
    rows_copy.start()
    own_rows = pltpu.make_async_copy(grad_ref.at[:, columns(core)], rows_ref.at[place], local_sem.at[0])
    own_rows.start()
    near = [
        pltpu.make_async_copy(far_ref, near_ref, near_sem.at[i])
        for i, (far_ref, near_ref) in enumerate(
            ((table_ref, near_table), (m1_ref, near_m1), (m2_ref, near_m2))
        )
    ]

    ids_copy.wait()
    mine, other = ids_ref[...], other_ids_ref[...]
    ids = jnp.concatenate(
        [jnp.where(core == 0, mine, other), jnp.where(core == 0, other, mine)], axis=1
    ).astype(jnp.float32)
    slot, slot_first, ids_down, most = find_slots(ids, slabs, slab_rows)

    count_ref[...] = jnp.broadcast_to(most.astype(jnp.int32), count_ref.shape)
    count_copies = []
    for d, twin in enumerate(twins):
        copy = pltpu.make_async_remote_copy(
            count_ref, got_count_ref.at[d], count_send.at[d], count_recv.at[d],
            device_id=twin, device_id_type=MESH,
        )
        copy.start()
        count_copies.append(copy)

    gather = (
        lax.broadcasted_iota(jnp.int32, (slots, 2 * tokens), 0) == slot.astype(jnp.int32)
    ).astype(jnp.float32).astype(jnp.bfloat16)
    own_rows.wait()
    rows_copy.wait()
    step = min(half, 512)

    @pl.loop(0, half // step)
    def _(c):
        at = pl.ds(pl.multiple_of(c * step, step), step)
        send_ref[:, at] = jnp.dot(
            gather, rows_ref[:, at], preferred_element_type=jnp.float32
        ).astype(jnp.bfloat16)

    def block(k):
        return pl.ds(pl.multiple_of(k * BLOCK_ROWS, BLOCK_ROWS), BLOCK_ROWS)

    block_copies = []
    for d, peer in enumerate(peers):
        copy = pltpu.make_async_remote_copy(
            send_ref.at[block(peer)], got_ref.at[block(me)], block_send.at[d], block_recv.at[d],
            device_id=(group, peer, core), device_id_type=MESH,
        )
        copy.start()
        block_copies.append(copy)
    own_block = pltpu.make_async_copy(
        send_ref.at[block(me)], got_ref.at[block(me)], local_sem.at[1]
    )
    own_block.start()
    for copy in near:
        copy.start()

    for d, copy in enumerate(count_copies):
        copy.wait()
        most = jnp.maximum(most, got_count_ref[d, 0:1, 0:1].astype(jnp.float32))
    row = lax.broadcasted_iota(jnp.int32, (2 * tokens, 2 * tokens), 0)
    lane = lax.broadcasted_iota(jnp.int32, (2 * tokens, 2 * tokens), 1)
    slot_down = jnp.sum(jnp.where(row == lane, slot_first, 0.0), axis=1, keepdims=True)
    lane = lax.broadcasted_iota(jnp.int32, (2 * tokens, LANES), 1)
    sub = lax.broadcasted_iota(jnp.int32, (8, LANES), 0)
    slot_down = slot_down.astype(jnp.int32)
    for k in range(slabs):
        chosen = (slot_down == lane + k * BLOCK_ROWS) & (lane < BLOCK_ROWS)
        note = jnp.sum(jnp.where(chosen, ids_down + 1.0, 0.0), axis=0, keepdims=True) - 1.0
        note_ref[k] = jnp.where(sub == 0, note, most).astype(jnp.int32)
    note_copies = []
    for d, peer in enumerate(peers):
        copy = pltpu.make_async_remote_copy(
            note_ref.at[peer], got_note_ref.at[me], note_send.at[d], note_recv.at[d],
            device_id=(group, peer, core), device_id_type=MESH,
        )
        copy.start()
        note_copies.append(copy)
    own_note = pltpu.make_async_copy(note_ref.at[me], got_note_ref.at[me], local_sem.at[2])
    own_note.start()
    own_note.wait()
    for copy in note_copies:
        copy.wait()

    row = lax.broadcasted_iota(jnp.int32, (BLOCK_ROWS, LANES), 0)
    lane = lax.broadcasted_iota(jnp.int32, (BLOCK_ROWS, LANES), 1)
    wide_row = lax.broadcasted_iota(jnp.int32, (BLOCK_ROWS, slots), 0)
    wide_lane = lax.broadcasted_iota(jnp.int32, (BLOCK_ROWS, slots), 1)
    got_ids = jnp.zeros((1, slots), jnp.float32)
    for k in range(slabs):
        note = got_note_ref[k].astype(jnp.float32)
        most = jnp.maximum(most, note[1:2, 0:1])
        down = jnp.sum(jnp.where(row == lane, note[0:1], 0.0), axis=1, keepdims=True)
        got_ids += jnp.sum(
            jnp.where(wide_lane == wide_row + k * BLOCK_ROWS, down, 0.0), axis=0, keepdims=True
        )
    got_ids_ref[...] = jnp.broadcast_to(got_ids.astype(jnp.int32), got_ids_ref.shape)
    most_ref[...] = jnp.broadcast_to(most.astype(jnp.int32), most_ref.shape)

    for copy in near:
        copy.wait()
    own_block.wait()
    for copy in block_copies:
        copy.wait()


def route(out_grad, token_ids, table, moment1, moment2, groups, slabs):
    tokens, width = out_grad.shape
    slots = slabs * BLOCK_ROWS
    half = width // 2
    ids = token_ids.reshape(1, tokens)
    vmem = pl.BlockSpec(memory_space=pltpu.VMEM)
    anywhere = pl.BlockSpec(memory_space=pl.ANY)
    dma = pltpu.SemaphoreType.DMA
    others = max(groups - 1, 1)
    return pl.pallas_call(
        functools.partial(route_kernel, groups, slabs, table.shape[0]),
        out_shape=(
            jax.ShapeDtypeStruct((slots, half), jnp.bfloat16),
            jax.ShapeDtypeStruct((8, slots), jnp.int32),
            jax.ShapeDtypeStruct((8, LANES), jnp.int32),
        ) + (jax.ShapeDtypeStruct(table.shape, jnp.float32),) * 3,
        in_specs=[vmem] + [anywhere] * 4,
        out_specs=(anywhere, vmem, vmem) + (anywhere,) * 3,
        scratch_shapes=[
            pltpu.VMEM((2 * tokens, half), jnp.bfloat16),
            pltpu.VMEM((1, tokens), jnp.int32),
            pltpu.VMEM((slots, half), jnp.bfloat16),
            pltpu.VMEM((slabs, 8, LANES), jnp.int32),
            pltpu.VMEM((slabs, 8, LANES), jnp.int32),
            pltpu.VMEM((8, LANES), jnp.int32),
            pltpu.VMEM((others, 8, LANES), jnp.int32),
            dma((3,)),
            dma((3,)),
            dma((2,)),
            dma((2,)),
            dma((others,)),
            dma((others,)),
            dma((slabs - 1,)),
            dma((slabs - 1,)),
            dma((slabs - 1,)),
            dma((slabs - 1,)),
        ],
        compiler_params=pltpu.CompilerParams(
            collective_id=0, has_side_effects=True, vmem_limit_bytes=16 * 1024 * 1024
        ),
        cost_estimate=pl.CostEstimate(
            flops=4 * slots * tokens * half, bytes_accessed=60_000_000, transcendentals=0
        ),
        name="route_rows",
    )(ids, out_grad, table, moment1, moment2)


def adam_kernel(
    ids_ref, got_ref, table_ref, m1_ref, m2_ref, t_out, m1_out, m2_out, onehot_ref, new_ref, sem
):
    slab_rows, half = table_ref.shape
    step = min(half, 256)
    first = lax.axis_index("vocab") * slab_rows
    row = lax.broadcasted_iota(jnp.int32, onehot_ref.shape, 0) + first
    onehot_ref[...] = (row == ids_ref[0:1, :]).astype(jnp.float32).astype(jnp.bfloat16)

    def copies(c):
        at = pl.ds(pl.multiple_of(c * step, step), step)
        return [
            pltpu.make_async_copy(new_ref.at[i, :, at], out.at[:, at], sem.at[i, c])
            for i, out in enumerate((t_out, m1_out, m2_out))
        ]

    @pl.loop(0, half // step)
    def _(c):
        at = pl.ds(pl.multiple_of(c * step, step), step)
        grad = jnp.dot(onehot_ref[...], got_ref[:, at], preferred_element_type=jnp.float32)
        new_values = adam(grad, table_ref[:, at], m1_ref[:, at], m2_ref[:, at])
        for i, value in enumerate(new_values):
            new_ref[i, :, at] = value
        for copy in copies(c):
            copy.start()

    @pl.loop(0, half // step)
    def _(c):
        for copy in copies(c):
            copy.wait()


def update(got, got_ids, table, moment1, moment2):
    slab_rows, half = table.shape
    slots = got.shape[0]
    shape = jax.ShapeDtypeStruct(table.shape, jnp.float32)
    return pl.pallas_call(
        adam_kernel,
        out_shape=(shape,) * 3,
        in_specs=[pl.BlockSpec(memory_space=pltpu.VMEM)] * 5,
        out_specs=(pl.BlockSpec(memory_space=pl.ANY),) * 3,
        scratch_shapes=[
            pltpu.VMEM((slab_rows, slots), jnp.bfloat16),
            pltpu.VMEM((3, slab_rows, half), jnp.float32),
            pltpu.SemaphoreType.DMA((3, half // min(half, 256))),
        ],
        compiler_params=pltpu.CompilerParams(vmem_limit_bytes=30 * 1024 * 1024),
        cost_estimate=pl.CostEstimate(
            flops=2 * slab_rows * slots * half,
            bytes_accessed=24 * slab_rows * half,
            transcendentals=slab_rows * half,
        ),
        name="adam_update",
    )(got_ids, got, table, moment1, moment2)


def per_device(groups, slabs, out_grad, token_ids, table, moment1, moment2):
    got, got_ids, most, *near = route(out_grad, token_ids, table, moment1, moment2, groups, slabs)
    outs = update(got, got_ids, *near)

    def again(carry):
        return (jnp.int32(0),) + dense_update(out_grad, token_ids, table, moment1, moment2)

    return lax.while_loop(lambda carry: carry[0] > BLOCK_ROWS, again, (most[0, 0],) + tuple(outs))[1:]


def solution(mesh):
    slab = P(("groups", "vocab"), "seq")
    return jax.shard_map(
        functools.partial(per_device, mesh.shape["groups"], mesh.shape["vocab"]),
        mesh=mesh,
        in_specs=(
            P(("groups", "vocab", "seq"), None), P(("groups", "vocab", "seq")), slab, slab, slab,
        ),
        out_specs=(slab, slab, slab),
        check_vma=False,
    )
```

```python
import functools

import jax
import jax.numpy as jnp
from jax import lax
from jax.experimental import pallas as pl
from jax.experimental.pallas import tpu as pltpu
from jax.sharding import PartitionSpec as P

STEP = 10
BLOCK_ROWS = 48
FAR_ROWS = 32
SPILL_ROWS = BLOCK_ROWS - FAR_ROWS
CHUNKS = 2
LANES = 128
FIRST_FIX = 1.0 - 0.9**STEP
SECOND_FIX = 1.0 - 0.999**STEP
MESH = pl.DeviceIdType.MESH


def adam(grad, table, moment1, moment2):
    new_moment1 = 0.9 * moment1 + 0.1 * grad
    new_moment2 = 0.999 * moment2 + 0.001 * grad * grad
    new_table = table - new_moment1 * (0.001 / FIRST_FIX) / (
        jnp.sqrt(new_moment2 * (1.0 / SECOND_FIX)) + 1e-08
    )
    return new_table, new_moment1, new_moment2


def dense_update(out_grad, token_ids, table, moment1, moment2):
    slab_rows = table.shape[0]
    slab_ids = lax.axis_index("vocab") * slab_rows + lax.iota(jnp.int32, slab_rows)
    grad_rows = lax.all_gather(out_grad, "vocab", axis=0, tiled=True)
    row_ids = lax.all_gather(token_ids, "vocab", axis=0, tiled=True)
    onehot = (slab_ids[:, None] == row_ids[None, :]).astype(jnp.bfloat16)
    partial_value = jnp.dot(onehot, grad_rows, preferred_element_type=jnp.float32)
    grad = lax.psum_scatter(
        partial_value.astype(jnp.bfloat16), "seq", scatter_dimension=1, tiled=True
    ).astype(jnp.float32)
    return adam(grad, table, moment1, moment2)


def find_slots(ids, me, slabs, slab_rows):
    tokens = ids.shape[1]
    row = lax.broadcasted_iota(jnp.int32, (tokens, tokens), 0)
    lane = lax.broadcasted_iota(jnp.int32, (tokens, tokens), 1)
    ids_down = jnp.sum(jnp.where(row == lane, ids, 0.0), axis=1, keepdims=True)
    same = jnp.where(ids_down == ids, 1.0, 0.0)
    before = jnp.where(row < lane, 1.0, 0.0)
    first = 1.0 - jnp.max(same * before, axis=0, keepdims=True)
    slab = jnp.zeros_like(ids)
    for k in range(1, slabs):
        slab += jnp.where(ids >= float(k * slab_rows), 1.0, 0.0)

    member = jnp.where(
        slab == lax.broadcasted_iota(jnp.int32, (slabs, tokens), 0).astype(jnp.float32), first, 0.0
    )
    ahead = jnp.dot(
        member.astype(jnp.bfloat16), before.astype(jnp.bfloat16),
        preferred_element_type=jnp.float32,
    )
    rank = jnp.sum(member * ahead, axis=0, keepdims=True)
    split = lax.convert_element_type(me // (slabs // 2), jnp.float32)
    partner = lax.convert_element_type(lax.rem(me + slabs // 2, slabs), jnp.float32)
    far = jnp.where(jnp.where(slab >= float(slabs // 2), 1.0, 0.0) == split, 0.0, 1.0)
    direct = jnp.where(rank < float(BLOCK_ROWS) - far * float(SPILL_ROWS), first, 0.0)
    spilled = (first - direct) * far
    spill_rank = jnp.dot(
        jnp.broadcast_to(spilled, (8, tokens)).astype(jnp.bfloat16), before.astype(jnp.bfloat16),
        preferred_element_type=jnp.float32,
    )[0:1]
    spilled = jnp.where(spill_rank < float(SPILL_ROWS), spilled, 0.0)
    fits = direct + spilled
    lost = jnp.max(first - fits, axis=1, keepdims=True)
    region = direct * slab + spilled * partner
    offset = direct * rank + spilled * (float(FAR_ROWS) + spill_rank)
    slot_first = fits * (region * float(BLOCK_ROWS) + offset + 1.0) - 1.0

    field = lax.broadcasted_iota(jnp.int32, (8, tokens), 0)
    facts = jnp.where(
        field == 0, region, jnp.where(field == 1, offset, jnp.where(field == 2, fits, 0.0))
    )
    facts = jnp.dot(
        facts.astype(jnp.bfloat16), same.astype(jnp.bfloat16), preferred_element_type=jnp.float32
    )
    slot = facts[0:1] * float(BLOCK_ROWS) + facts[1:2] + facts[2:3] - 1.0
    return slot, slot_first, ids_down, lost


def paired(me, d, count):
    bits = [lax.rem(me // (1 << k), 2) for k in range(count.bit_length() - 1)]
    return sum((1 - bit if d >> k & 1 else bit) * (1 << k) for k, bit in enumerate(bits))


def route_kernel(
    groups, slabs, slab_rows,
    ids_ref, grad_ref, table_ref, m1_ref, m2_ref,
    got_ref, got_ids_ref, most_ref, near_table, near_m1, near_m2,
    rows_ref, other_ids_ref, send_ref, note_ref, got_note_ref, count_ref, got_count_ref,
    local_sem, near_sem, pair_send, pair_recv, count_send, count_recv,
    note_send, note_recv, block_send, block_recv, spill_send, spill_recv,
):
    tokens, width = grad_ref.shape
    half = width // 2
    slots = slabs * BLOCK_ROWS
    group, me, core = lax.axis_index("groups"), lax.axis_index("vocab"), lax.axis_index("seq")
    sibling = (group, me, 1 - core)
    twins = [(lax.rem(group + d, groups), me, core) for d in range(1, groups)]
    across = slabs // 2
    steps = [across] + list(range(across + 1, slabs)) + list(range(1, across))
    peers = [paired(me, d, slabs) for d in steps]

    barrier = pltpu.get_barrier_semaphore()
    for device in [sibling] + twins + [(group, peer, core) for peer in peers]:
        pl.semaphore_signal(barrier, inc=1, device_id=device, device_id_type=MESH)
    pl.semaphore_wait(barrier, groups + slabs - 1)

    def columns(which):
        return pl.ds(pl.multiple_of(which * half, half), half)

    place = pl.ds(pl.multiple_of(core * tokens, tokens), tokens)
    ids_copy = pltpu.make_async_remote_copy(
        ids_ref, other_ids_ref, pair_send.at[0], pair_recv.at[0],
        device_id=sibling, device_id_type=MESH,
    )
    ids_copy.start()
    rows_copy = pltpu.make_async_remote_copy(
        grad_ref.at[:, columns(1 - core)], rows_ref.at[place], pair_send.at[1], pair_recv.at[1],
        device_id=sibling, device_id_type=MESH,
    )
    rows_copy.start()
    own_rows = pltpu.make_async_copy(grad_ref.at[:, columns(core)], rows_ref.at[place], local_sem.at[0])
    own_rows.start()
    near = [
        pltpu.make_async_copy(far_ref, near_ref, near_sem.at[i])
        for i, (far_ref, near_ref) in enumerate(
            ((table_ref, near_table), (m1_ref, near_m1), (m2_ref, near_m2))
        )
    ]

    ids_copy.wait()
    mine, other = ids_ref[...], other_ids_ref[...]
    ids = jnp.concatenate(
        [jnp.where(core == 0, mine, other), jnp.where(core == 0, other, mine)], axis=1
    ).astype(jnp.float32)
    slot, slot_first, ids_down, most = find_slots(ids, me, slabs, slab_rows)

    count_ref[...] = jnp.broadcast_to(most.astype(jnp.int32), count_ref.shape)
    count_copies = []
    for d, twin in enumerate(twins):
        copy = pltpu.make_async_remote_copy(
            count_ref, got_count_ref.at[d], count_send.at[d], count_recv.at[d],
            device_id=twin, device_id_type=MESH,
        )
        copy.start()
        count_copies.append(copy)

    gather = (
        lax.broadcasted_iota(jnp.int32, (slots, 2 * tokens), 0) == slot.astype(jnp.int32)
    ).astype(jnp.float32).astype(jnp.bfloat16)
    own_rows.wait()
    rows_copy.wait()
    step = half // CHUNKS

    def block(k, start=0, rows=BLOCK_ROWS):
        return pl.ds(pl.multiple_of(k * BLOCK_ROWS + start, 16), rows)

    block_copies = []
    for c in range(CHUNKS):
        at = slice(c * step, (c + 1) * step)
        send_ref[:, at] = jnp.dot(
            gather, rows_ref[:, at], preferred_element_type=jnp.float32
        ).astype(jnp.bfloat16)
        for d, peer in enumerate(peers):
            rows = FAR_ROWS if steps[d] > across else BLOCK_ROWS
            copy = pltpu.make_async_remote_copy(
                send_ref.at[block(peer, 0, rows), at], got_ref.at[block(me, 0, rows), at],
                block_send.at[c, d], block_recv.at[c, d],
                device_id=(group, peer, core), device_id_type=MESH,
            )
            copy.start()
            block_copies.append(copy)
    own_block = pltpu.make_async_copy(
        send_ref.at[block(me)], got_ref.at[block(me)], local_sem.at[1]
    )
    own_block.start()
    for copy in near:
        copy.start()

    for d, copy in enumerate(count_copies):
        copy.wait()
        most = jnp.maximum(most, got_count_ref[d, 0:1, 0:1].astype(jnp.float32))
    row = lax.broadcasted_iota(jnp.int32, (2 * tokens, 2 * tokens), 0)
    lane = lax.broadcasted_iota(jnp.int32, (2 * tokens, 2 * tokens), 1)
    slot_down = jnp.sum(jnp.where(row == lane, slot_first, 0.0), axis=1, keepdims=True)
    lane = lax.broadcasted_iota(jnp.int32, (2 * tokens, LANES), 1)
    sub = lax.broadcasted_iota(jnp.int32, (8, LANES), 0)
    slot_down = slot_down.astype(jnp.int32)
    for k in range(slabs):
        region = jnp.where((k // across != me // across) & (lane >= FAR_ROWS), peers[0], k)
        chosen = (slot_down == lane + region * BLOCK_ROWS) & (lane < BLOCK_ROWS)
        note = jnp.sum(jnp.where(chosen, ids_down + 1.0, 0.0), axis=0, keepdims=True) - 1.0
        note_ref[k] = jnp.where(sub == 0, note, most).astype(jnp.int32)
    note_copies = []
    for d, peer in enumerate(peers):
        copy = pltpu.make_async_remote_copy(
            note_ref.at[peer], got_note_ref.at[me], note_send.at[d], note_recv.at[d],
            device_id=(group, peer, core), device_id_type=MESH,
        )
        copy.start()
        note_copies.append(copy)
    own_note = pltpu.make_async_copy(note_ref.at[me], got_note_ref.at[me], local_sem.at[2])
    own_note.start()
    own_note.wait()

    spill_copies = []
    for c in range(CHUNKS):
        at = slice(c * step, (c + 1) * step)
        block_copies[c * len(peers)].wait()
        shared = block(peers[0], FAR_ROWS, SPILL_ROWS)
        for d in range(1, across):
            copy = pltpu.make_async_remote_copy(
                got_ref.at[shared, at], got_ref.at[shared, at],
                spill_send.at[c, d - 1], spill_recv.at[c, d - 1],
                device_id=(group, paired(me, d, slabs), core), device_id_type=MESH,
            )
            copy.start()
            spill_copies.append(copy)
    for copy in note_copies:
        copy.wait()

    row = lax.broadcasted_iota(jnp.int32, (BLOCK_ROWS, LANES), 0)
    lane = lax.broadcasted_iota(jnp.int32, (BLOCK_ROWS, LANES), 1)
    wide_row = lax.broadcasted_iota(jnp.int32, (BLOCK_ROWS, slots), 0)
    wide_lane = lax.broadcasted_iota(jnp.int32, (BLOCK_ROWS, slots), 1)
    got_ids = jnp.zeros((1, slots), jnp.float32)
    for k in range(slabs):
        note = got_note_ref[k].astype(jnp.float32)
        most = jnp.maximum(most, note[1:2, 0:1])
        down = jnp.sum(jnp.where(row == lane, note[0:1], 0.0), axis=1, keepdims=True)
        got_ids += jnp.sum(
            jnp.where(wide_lane == wide_row + k * BLOCK_ROWS, down, 0.0), axis=0, keepdims=True
        )
    got_ids_ref[...] = jnp.broadcast_to(got_ids.astype(jnp.int32), got_ids_ref.shape)
    most_ref[...] = jnp.broadcast_to(most.astype(jnp.int32), most_ref.shape)

    for copy in near:
        copy.wait()
    own_block.wait()
    for at, copy in enumerate(block_copies):
        if at % len(peers):
            copy.wait()
    for copy in spill_copies:
        copy.wait()


def route(out_grad, token_ids, table, moment1, moment2, groups, slabs):
    tokens, width = out_grad.shape
    slots = slabs * BLOCK_ROWS
    half = width // 2
    ids = token_ids.reshape(1, tokens)
    vmem = pl.BlockSpec(memory_space=pltpu.VMEM)
    anywhere = pl.BlockSpec(memory_space=pl.ANY)
    dma = pltpu.SemaphoreType.DMA
    others = max(groups - 1, 1)
    return pl.pallas_call(
        functools.partial(route_kernel, groups, slabs, table.shape[0]),
        out_shape=(
            jax.ShapeDtypeStruct((slots, half), jnp.bfloat16),
            jax.ShapeDtypeStruct((8, slots), jnp.int32),
            jax.ShapeDtypeStruct((8, LANES), jnp.int32),
        ) + (jax.ShapeDtypeStruct(table.shape, jnp.float32),) * 3,
        in_specs=[vmem] + [anywhere] * 4,
        out_specs=(anywhere, vmem, vmem) + (anywhere,) * 3,
        scratch_shapes=[
            pltpu.VMEM((2 * tokens, half), jnp.bfloat16),
            pltpu.VMEM((1, tokens), jnp.int32),
            pltpu.VMEM((slots, half), jnp.bfloat16),
            pltpu.VMEM((slabs, 8, LANES), jnp.int32),
            pltpu.VMEM((slabs, 8, LANES), jnp.int32),
            pltpu.VMEM((8, LANES), jnp.int32),
            pltpu.VMEM((others, 8, LANES), jnp.int32),
            dma((3,)),
            dma((3,)),
            dma((2,)),
            dma((2,)),
            dma((others,)),
            dma((others,)),
            dma((slabs - 1,)),
            dma((slabs - 1,)),
            dma((CHUNKS, slabs - 1)),
            dma((CHUNKS, slabs - 1)),
            dma((CHUNKS, slabs // 2 - 1)),
            dma((CHUNKS, slabs // 2 - 1)),
        ],
        compiler_params=pltpu.CompilerParams(
            collective_id=0, has_side_effects=True, vmem_limit_bytes=16 * 1024 * 1024
        ),
        cost_estimate=pl.CostEstimate(
            flops=4 * slots * tokens * half, bytes_accessed=60_000_000, transcendentals=0
        ),
        name="route_rows",
    )(ids, out_grad, table, moment1, moment2)


def adam_kernel(
    ids_ref, got_ref, table_ref, m1_ref, m2_ref, t_out, m1_out, m2_out, onehot_ref, new_ref, sem
):
    slab_rows, half = table_ref.shape
    step = min(half, 256)
    first = lax.axis_index("vocab") * slab_rows
    row = lax.broadcasted_iota(jnp.int32, onehot_ref.shape, 0) + first
    onehot_ref[...] = (row == ids_ref[0:1, :]).astype(jnp.float32).astype(jnp.bfloat16)

    def copies(c):
        at = pl.ds(pl.multiple_of(c * step, step), step)
        return [
            pltpu.make_async_copy(new_ref.at[i, :, at], out.at[:, at], sem.at[i, c])
            for i, out in enumerate((t_out, m1_out, m2_out))
        ]

    @pl.loop(0, half // step)
    def _(c):
        at = pl.ds(pl.multiple_of(c * step, step), step)
        grad = jnp.dot(onehot_ref[...], got_ref[:, at], preferred_element_type=jnp.float32)
        new_values = adam(grad, table_ref[:, at], m1_ref[:, at], m2_ref[:, at])
        for i, value in enumerate(new_values):
            new_ref[i, :, at] = value
        for copy in copies(c):
            copy.start()

    @pl.loop(0, half // step)
    def _(c):
        for copy in copies(c):
            copy.wait()


def update(got, got_ids, table, moment1, moment2):
    slab_rows, half = table.shape
    slots = got.shape[0]
    shape = jax.ShapeDtypeStruct(table.shape, jnp.float32)
    return pl.pallas_call(
        adam_kernel,
        out_shape=(shape,) * 3,
        in_specs=[pl.BlockSpec(memory_space=pltpu.VMEM)] * 5,
        out_specs=(pl.BlockSpec(memory_space=pl.ANY),) * 3,
        scratch_shapes=[
            pltpu.VMEM((slab_rows, slots), jnp.bfloat16),
            pltpu.VMEM((3, slab_rows, half), jnp.float32),
            pltpu.SemaphoreType.DMA((3, half // min(half, 256))),
        ],
        compiler_params=pltpu.CompilerParams(vmem_limit_bytes=30 * 1024 * 1024),
        cost_estimate=pl.CostEstimate(
            flops=2 * slab_rows * slots * half,
            bytes_accessed=24 * slab_rows * half,
            transcendentals=slab_rows * half,
        ),
        name="adam_update",
    )(got_ids, got, table, moment1, moment2)


def per_device(groups, slabs, out_grad, token_ids, table, moment1, moment2):
    got, got_ids, most, *near = route(out_grad, token_ids, table, moment1, moment2, groups, slabs)
    outs = update(got, got_ids, *near)

    def again(carry):
        return (jnp.int32(0),) + dense_update(out_grad, token_ids, table, moment1, moment2)

    return lax.while_loop(lambda carry: carry[0] > 0, again, (most[0, 0],) + tuple(outs))[1:]


def solution(mesh):
    slab = P(("groups", "vocab"), "seq")
    return jax.shard_map(
        functools.partial(per_device, mesh.shape["groups"], mesh.shape["vocab"]),
        mesh=mesh,
        in_specs=(
            P(("groups", "vocab", "seq"), None), P(("groups", "vocab", "seq")), slab, slab, slab,
        ),
        out_specs=(slab, slab, slab),
        check_vma=False,
    )
```

```python
import functools

import jax
import jax.numpy as jnp
from jax import lax
from jax.experimental import pallas as pl
from jax.experimental.pallas import tpu as pltpu
from jax.sharding import PartitionSpec as P

STEP = 10
BLOCK_ROWS = 48
FAR_ROWS = 32
SPILL_ROWS = BLOCK_ROWS - FAR_ROWS
CHUNKS = 2
LANES = 128
FIRST_FIX = 1.0 - 0.9**STEP
SECOND_FIX = 1.0 - 0.999**STEP
MESH = pl.DeviceIdType.MESH


def adam(grad, table, moment1, moment2):
    new_moment1 = 0.9 * moment1 + 0.1 * grad
    new_moment2 = 0.999 * moment2 + 0.001 * grad * grad
    new_table = table - new_moment1 * (0.001 / FIRST_FIX) / (
        jnp.sqrt(new_moment2 * (1.0 / SECOND_FIX)) + 1e-08
    )
    return new_table, new_moment1, new_moment2


def dense_update(out_grad, token_ids, table, moment1, moment2):
    slab_rows = table.shape[0]
    slab_ids = lax.axis_index("vocab") * slab_rows + lax.iota(jnp.int32, slab_rows)
    grad_rows = lax.all_gather(out_grad, "vocab", axis=0, tiled=True)
    row_ids = lax.all_gather(token_ids, "vocab", axis=0, tiled=True)
    onehot = (slab_ids[:, None] == row_ids[None, :]).astype(jnp.bfloat16)
    partial_value = jnp.dot(onehot, grad_rows, preferred_element_type=jnp.float32)
    grad = lax.psum_scatter(
        partial_value.astype(jnp.bfloat16), "seq", scatter_dimension=1, tiled=True
    ).astype(jnp.float32)
    return adam(grad, table, moment1, moment2)


def find_slots(ids, me, slabs, slab_rows):
    tokens = ids.shape[1]
    row = lax.broadcasted_iota(jnp.int32, (tokens, tokens), 0)
    lane = lax.broadcasted_iota(jnp.int32, (tokens, tokens), 1)
    ids_down = jnp.sum(jnp.where(row == lane, ids, 0.0), axis=1, keepdims=True)
    same = jnp.where(ids_down == ids, 1.0, 0.0)
    before = jnp.where(row < lane, 1.0, 0.0)
    first = 1.0 - jnp.max(same * before, axis=0, keepdims=True)
    slab = jnp.zeros_like(ids)
    for k in range(1, slabs):
        slab += jnp.where(ids >= float(k * slab_rows), 1.0, 0.0)

    member = jnp.where(
        slab == lax.broadcasted_iota(jnp.int32, (slabs, tokens), 0).astype(jnp.float32), first, 0.0
    )
    ahead = jnp.dot(
        member.astype(jnp.bfloat16), before.astype(jnp.bfloat16),
        preferred_element_type=jnp.float32,
    )
    rank = jnp.sum(member * ahead, axis=0, keepdims=True)
    split = lax.convert_element_type(me // (slabs // 2), jnp.float32)
    partner = lax.convert_element_type(lax.rem(me + slabs // 2, slabs), jnp.float32)
    far = jnp.where(jnp.where(slab >= float(slabs // 2), 1.0, 0.0) == split, 0.0, 1.0)
    direct = jnp.where(rank < float(BLOCK_ROWS) - far * float(SPILL_ROWS), first, 0.0)
    spilled = (first - direct) * far
    spill_rank = jnp.dot(
        jnp.broadcast_to(spilled, (8, tokens)).astype(jnp.bfloat16), before.astype(jnp.bfloat16),
        preferred_element_type=jnp.float32,
    )[0:1]
    spilled = jnp.where(spill_rank < float(SPILL_ROWS), spilled, 0.0)
    fits = direct + spilled
    lost = jnp.max(first - fits, axis=1, keepdims=True)
    region = direct * slab + spilled * partner
    offset = direct * rank + spilled * (float(FAR_ROWS) + spill_rank)
    slot_first = fits * (region * float(BLOCK_ROWS) + offset + 1.0) - 1.0

    field = lax.broadcasted_iota(jnp.int32, (8, tokens), 0)
    facts = jnp.where(
        field == 0, region, jnp.where(field == 1, offset, jnp.where(field == 2, fits, 0.0))
    )
    facts = jnp.dot(
        facts.astype(jnp.bfloat16), same.astype(jnp.bfloat16), preferred_element_type=jnp.float32
    )
    slot = facts[0:1] * float(BLOCK_ROWS) + facts[1:2] + facts[2:3] - 1.0
    return slot, slot_first, ids_down, lost


def paired(me, d, count):
    bits = [lax.rem(me // (1 << k), 2) for k in range(count.bit_length() - 1)]
    return sum((1 - bit if d >> k & 1 else bit) * (1 << k) for k, bit in enumerate(bits))


def route_kernel(
    groups, slabs, slab_rows,
    ids_ref, grad_ref, table_ref, m1_ref, m2_ref,
    got_ref, got_ids_ref, most_ref, near_table, near_m1, near_m2,
    rows_ref, other_ids_ref, send_ref, note_ref, got_note_ref, count_ref, got_count_ref,
    local_sem, near_sem, pair_send, pair_recv, count_send, count_recv,
    note_send, note_recv, block_send, block_recv, spill_send, spill_recv,
):
    tokens, width = grad_ref.shape
    half = width // 2
    slots = slabs * BLOCK_ROWS
    group, me, core = lax.axis_index("groups"), lax.axis_index("vocab"), lax.axis_index("seq")
    sibling = (group, me, 1 - core)
    twins = [(lax.rem(group + d, groups), me, core) for d in range(1, groups)]
    across = slabs // 2
    steps = [across] + list(range(across + 1, slabs)) + list(range(1, across))
    peers = [paired(me, d, slabs) for d in steps]

    def columns(which):
        return pl.ds(pl.multiple_of(which * half, half), half)

    place = pl.ds(pl.multiple_of(core * tokens, tokens), tokens)
    own_rows = pltpu.make_async_copy(grad_ref.at[:, columns(core)], rows_ref.at[place], local_sem.at[0])
    own_rows.start()

    barrier = pltpu.get_barrier_semaphore()
    for device in [sibling] + twins + [(group, peer, core) for peer in peers]:
        pl.semaphore_signal(barrier, inc=1, device_id=device, device_id_type=MESH)
    pl.semaphore_wait(barrier, groups + slabs - 1)

    ids_copy = pltpu.make_async_remote_copy(
        ids_ref, other_ids_ref, pair_send.at[0], pair_recv.at[0],
        device_id=sibling, device_id_type=MESH,
    )
    ids_copy.start()
    rows_copy = pltpu.make_async_remote_copy(
        grad_ref.at[:, columns(1 - core)], rows_ref.at[place], pair_send.at[1], pair_recv.at[1],
        device_id=sibling, device_id_type=MESH,
    )
    rows_copy.start()
    near = [
        pltpu.make_async_copy(far_ref, near_ref, near_sem.at[i])
        for i, (far_ref, near_ref) in enumerate(
            ((table_ref, near_table), (m1_ref, near_m1), (m2_ref, near_m2))
        )
    ]

    ids_copy.wait()
    mine, other = ids_ref[...], other_ids_ref[...]
    ids = jnp.concatenate(
        [jnp.where(core == 0, mine, other), jnp.where(core == 0, other, mine)], axis=1
    ).astype(jnp.float32)
    slot, slot_first, ids_down, most = find_slots(ids, me, slabs, slab_rows)

    count_ref[...] = jnp.broadcast_to(most.astype(jnp.int32), count_ref.shape)
    count_copies = []
    for d, twin in enumerate(twins):
        copy = pltpu.make_async_remote_copy(
            count_ref, got_count_ref.at[d], count_send.at[d], count_recv.at[d],
            device_id=twin, device_id_type=MESH,
        )
        copy.start()
        count_copies.append(copy)

    gather = (
        lax.broadcasted_iota(jnp.int32, (slots, 2 * tokens), 0) == slot.astype(jnp.int32)
    ).astype(jnp.float32).astype(jnp.bfloat16)
    own_rows.wait()
    rows_copy.wait()
    step = half // CHUNKS

    def block(k, start=0, rows=BLOCK_ROWS):
        return pl.ds(pl.multiple_of(k * BLOCK_ROWS + start, 16), rows)

    block_copies = {}

    def send(c, d):
        at = slice(c * step, (c + 1) * step)
        rows = FAR_ROWS if steps[d] > across else BLOCK_ROWS
        copy = pltpu.make_async_remote_copy(
            send_ref.at[block(peers[d], 0, rows), at], got_ref.at[block(me, 0, rows), at],
            block_send.at[c, d], block_recv.at[c, d],
            device_id=(group, peers[d], core), device_id_type=MESH,
        )
        copy.start()
        block_copies[c, d] = copy

    for c in range(CHUNKS):
        at = slice(c * step, (c + 1) * step)
        send_ref[:, at] = jnp.dot(
            gather, rows_ref[:, at], preferred_element_type=jnp.float32
        ).astype(jnp.bfloat16)
        for d in range(slabs - across):
            send(c, d)
    for c in range(CHUNKS):
        for d in range(slabs - across, len(peers)):
            send(c, d)
    own_block = pltpu.make_async_copy(
        send_ref.at[block(me)], got_ref.at[block(me)], local_sem.at[1]
    )
    own_block.start()
    for copy in near:
        copy.start()

    for d, copy in enumerate(count_copies):
        copy.wait()
        most = jnp.maximum(most, got_count_ref[d, 0:1, 0:1].astype(jnp.float32))
    row = lax.broadcasted_iota(jnp.int32, (2 * tokens, 2 * tokens), 0)
    lane = lax.broadcasted_iota(jnp.int32, (2 * tokens, 2 * tokens), 1)
    slot_down = jnp.sum(jnp.where(row == lane, slot_first, 0.0), axis=1, keepdims=True)
    lane = lax.broadcasted_iota(jnp.int32, (2 * tokens, LANES), 1)
    sub = lax.broadcasted_iota(jnp.int32, (8, LANES), 0)
    slot_down = slot_down.astype(jnp.int32)
    for k in range(slabs):
        region = jnp.where((k // across != me // across) & (lane >= FAR_ROWS), peers[0], k)
        chosen = (slot_down == lane + region * BLOCK_ROWS) & (lane < BLOCK_ROWS)
        note = jnp.sum(jnp.where(chosen, ids_down + 1.0, 0.0), axis=0, keepdims=True) - 1.0
        note_ref[k] = jnp.where(sub == 0, note, most).astype(jnp.int32)
    note_copies = []
    for d, peer in enumerate(peers):
        copy = pltpu.make_async_remote_copy(
            note_ref.at[peer], got_note_ref.at[me], note_send.at[d], note_recv.at[d],
            device_id=(group, peer, core), device_id_type=MESH,
        )
        copy.start()
        note_copies.append(copy)
    own_note = pltpu.make_async_copy(note_ref.at[me], got_note_ref.at[me], local_sem.at[2])
    own_note.start()
    own_note.wait()

    spill_copies = []
    for c in range(CHUNKS):
        at = slice(c * step, (c + 1) * step)
        block_copies[c, 0].wait()
        shared = block(peers[0], FAR_ROWS, SPILL_ROWS)
        for d in range(1, across):
            copy = pltpu.make_async_remote_copy(
                got_ref.at[shared, at], got_ref.at[shared, at],
                spill_send.at[c, d - 1], spill_recv.at[c, d - 1],
                device_id=(group, paired(me, d, slabs), core), device_id_type=MESH,
            )
            copy.start()
            spill_copies.append(copy)
    for copy in note_copies:
        copy.wait()

    row = lax.broadcasted_iota(jnp.int32, (BLOCK_ROWS, LANES), 0)
    lane = lax.broadcasted_iota(jnp.int32, (BLOCK_ROWS, LANES), 1)
    wide_row = lax.broadcasted_iota(jnp.int32, (BLOCK_ROWS, slots), 0)
    wide_lane = lax.broadcasted_iota(jnp.int32, (BLOCK_ROWS, slots), 1)
    got_ids = jnp.zeros((1, slots), jnp.float32)
    for k in range(slabs):
        note = got_note_ref[k].astype(jnp.float32)
        most = jnp.maximum(most, note[1:2, 0:1])
        down = jnp.sum(jnp.where(row == lane, note[0:1], 0.0), axis=1, keepdims=True)
        got_ids += jnp.sum(
            jnp.where(wide_lane == wide_row + k * BLOCK_ROWS, down, 0.0), axis=0, keepdims=True
        )
    got_ids_ref[...] = jnp.broadcast_to(got_ids.astype(jnp.int32), got_ids_ref.shape)
    most_ref[...] = jnp.broadcast_to(most.astype(jnp.int32), most_ref.shape)

    for copy in near:
        copy.wait()
    own_block.wait()
    for (_, d), copy in block_copies.items():
        if d:
            copy.wait()
    for copy in spill_copies:
        copy.wait()


def route(out_grad, token_ids, table, moment1, moment2, groups, slabs):
    tokens, width = out_grad.shape
    slots = slabs * BLOCK_ROWS
    half = width // 2
    ids = token_ids.reshape(1, tokens)
    vmem = pl.BlockSpec(memory_space=pltpu.VMEM)
    anywhere = pl.BlockSpec(memory_space=pl.ANY)
    dma = pltpu.SemaphoreType.DMA
    others = max(groups - 1, 1)
    return pl.pallas_call(
        functools.partial(route_kernel, groups, slabs, table.shape[0]),
        out_shape=(
            jax.ShapeDtypeStruct((slots, half), jnp.bfloat16),
            jax.ShapeDtypeStruct((8, slots), jnp.int32),
            jax.ShapeDtypeStruct((8, LANES), jnp.int32),
        ) + (jax.ShapeDtypeStruct(table.shape, jnp.float32),) * 3,
        in_specs=[vmem] + [anywhere] * 4,
        out_specs=(anywhere, vmem, vmem) + (anywhere,) * 3,
        scratch_shapes=[
            pltpu.VMEM((2 * tokens, half), jnp.bfloat16),
            pltpu.VMEM((1, tokens), jnp.int32),
            pltpu.VMEM((slots, half), jnp.bfloat16),
            pltpu.VMEM((slabs, 8, LANES), jnp.int32),
            pltpu.VMEM((slabs, 8, LANES), jnp.int32),
            pltpu.VMEM((8, LANES), jnp.int32),
            pltpu.VMEM((others, 8, LANES), jnp.int32),
            dma((3,)),
            dma((3,)),
            dma((2,)),
            dma((2,)),
            dma((others,)),
            dma((others,)),
            dma((slabs - 1,)),
            dma((slabs - 1,)),
            dma((CHUNKS, slabs - 1)),
            dma((CHUNKS, slabs - 1)),
            dma((CHUNKS, slabs // 2 - 1)),
            dma((CHUNKS, slabs // 2 - 1)),
        ],
        compiler_params=pltpu.CompilerParams(
            collective_id=0, has_side_effects=True, vmem_limit_bytes=16 * 1024 * 1024
        ),
        cost_estimate=pl.CostEstimate(
            flops=4 * slots * tokens * half, bytes_accessed=60_000_000, transcendentals=0
        ),
        name="route_rows",
    )(ids, out_grad, table, moment1, moment2)


def adam_kernel(
    ids_ref, got_ref, table_ref, m1_ref, m2_ref, t_out, m1_out, m2_out, onehot_ref, new_ref, sem
):
    slab_rows, half = table_ref.shape
    step = min(half, 512)
    first = lax.axis_index("vocab") * slab_rows
    row = lax.broadcasted_iota(jnp.int32, onehot_ref.shape, 0) + first
    onehot_ref[...] = (row == ids_ref[0:1, :]).astype(jnp.float32).astype(jnp.bfloat16)

    def copies(c):
        at = pl.ds(pl.multiple_of(c * step, step), step)
        return [
            pltpu.make_async_copy(new_ref.at[i, :, at], out.at[:, at], sem.at[i, c])
            for i, out in enumerate((t_out, m1_out, m2_out))
        ]

    @pl.loop(0, half // step)
    def _(c):
        at = pl.ds(pl.multiple_of(c * step, step), step)
        grad = jnp.dot(onehot_ref[...], got_ref[:, at], preferred_element_type=jnp.float32)
        new_values = adam(grad, table_ref[:, at], m1_ref[:, at], m2_ref[:, at])
        for i, value in enumerate(new_values):
            new_ref[i, :, at] = value
        for copy in copies(c):
            copy.start()

    @pl.loop(0, half // step)
    def _(c):
        for copy in copies(c):
            copy.wait()


def update(got, got_ids, table, moment1, moment2):
    slab_rows, half = table.shape
    slots = got.shape[0]
    shape = jax.ShapeDtypeStruct(table.shape, jnp.float32)
    return pl.pallas_call(
        adam_kernel,
        out_shape=(shape,) * 3,
        in_specs=[pl.BlockSpec(memory_space=pltpu.VMEM)] * 5,
        out_specs=(pl.BlockSpec(memory_space=pl.ANY),) * 3,
        scratch_shapes=[
            pltpu.VMEM((slab_rows, slots), jnp.bfloat16),
            pltpu.VMEM((3, slab_rows, half), jnp.float32),
            pltpu.SemaphoreType.DMA((3, half // min(half, 512))),
        ],
        compiler_params=pltpu.CompilerParams(vmem_limit_bytes=30 * 1024 * 1024),
        cost_estimate=pl.CostEstimate(
            flops=2 * slab_rows * slots * half,
            bytes_accessed=24 * slab_rows * half,
            transcendentals=slab_rows * half,
        ),
        name="adam_update",
    )(got_ids, got, table, moment1, moment2)


def per_device(groups, slabs, out_grad, token_ids, table, moment1, moment2):
    got, got_ids, most, *near = route(out_grad, token_ids, table, moment1, moment2, groups, slabs)
    outs = update(got, got_ids, *near)

    def again(carry):
        return (jnp.int32(0),) + dense_update(out_grad, token_ids, table, moment1, moment2)

    return lax.while_loop(lambda carry: carry[0] > 0, again, (most[0, 0],) + tuple(outs))[1:]


def solution(mesh):
    slab = P(("groups", "vocab"), "seq")
    return jax.shard_map(
        functools.partial(per_device, mesh.shape["groups"], mesh.shape["vocab"]),
        mesh=mesh,
        in_specs=(
            P(("groups", "vocab", "seq"), None), P(("groups", "vocab", "seq")), slab, slab, slab,
        ),
        out_specs=(slab, slab, slab),
        check_vma=False,
    )
```
